512 devices in a mesh: ctx: 64 (over x, z, core), head: 8 (over y).
Axes of the slice: x: 4, y: 8, z: 8, core: 2. Of those that a mesh axis runs over, the one named last changes fastest.
Arguments:
- queries: bfloat16 [32768, 4096], P('ctx', 'head'), may hold values from -6 to 6
- keys: bfloat16 [32768, 4096], P('ctx', 'head'), may hold values from -6 to 6
- values: bfloat16 [32768, 4096], P('ctx', 'head'), may hold values from -6 to 6
- out_grad: bfloat16 [32768, 4096], P(('ctx', 'head')), may hold values from -6 to 6
Outputs:
- query_grad: bfloat16 [32768, 4096], P('ctx', 'head')
- key_grad: bfloat16 [32768, 4096], P('ctx', 'head')
- value_grad: bfloat16 [32768, 4096], P('ctx', 'head')
The draws below stay inside these ranges and needn't reach their ends.
All inputs are finite; a program needn't handle non-finite values.
Results may differ from the reference program's by a relative error of at most 0.0049.
Values may be sent and summed in bfloat16 or wider, within the bound.
A program may use at most 128 MiB of HBM per device.

```python
import math
import jax
import jax.numpy as jnp
from jax import lax

HEADS = 32
HEAD_DIM = 128
TOK_DEV = 512
TOKENS = 32768


def steps_of(stream_key, shape, split, low, high):
    gain, own = 1.0, jax.random.fold_in(stream_key, 6)
    for dim, blocks in split:
        steps = jnp.exp(jax.random.uniform(jax.random.fold_in(own, dim), (blocks,), jnp.float32, low / len(split), high / len(split)))
        gain = gain * jnp.repeat(steps, shape[dim] // blocks).reshape([-1 if axis == dim else 1 for axis in range(len(shape))])
    return gain


def gaussian(rng, extent, spread, most, cuts=(), dtype=jnp.bfloat16):
    array = jax.random.normal(rng, extent, jnp.float32) * spread
    if len(cuts) > 0:
        array = steps_of(rng, extent, cuts, -0.22, 0.18) * array
    return jnp.clip(array, min=-most, max=most).astype(dtype)


def setup_inputs(seed: int = 0) -> dict:
    key_of = jax.random.split(jax.random.key(seed), 5)
    return {
        "queries": gaussian(key_of[0], (TOKENS, HEADS * HEAD_DIM), 1.0, 6.0, ((0, 64), (1, 8))),
        "keys": gaussian(key_of[1], (TOKENS, HEADS * HEAD_DIM), 1.0, 6.0, ((0, 64), (1, 8))),
        "values": gaussian(key_of[2], (TOKENS, HEADS * HEAD_DIM), 1.0, 6.0, ((0, 64), (1, 8))),
        "out_grad": gaussian(key_of[3], (TOKENS, HEADS * HEAD_DIM), 1.0, 6.0, ((0, 512),)),
    }


def group_grads(pieces):
    query_rows, key_rows, value_rows, grad_rows, key_state, grad_state = pieces
    length = query_rows.shape[0]
    causal = jnp.tril(jnp.ones((length, length), jnp.bool_))
    query_f = query_rows.astype(jnp.float32)
    key_f = key_rows.astype(jnp.float32)
    value_f = value_rows.astype(jnp.float32)
    grad_f = grad_rows.astype(jnp.float32)
    scores = jnp.einsum('ihd,jhd->hij', query_f, key_f)
    attend = jnp.where(causal[None], scores, 0.0).astype(jnp.bfloat16).astype(jnp.float32)
    mixed = jnp.einsum('ihe,jhe->hij', grad_f, value_f)
    upstream = jnp.where(causal[None], mixed, 0.0).astype(jnp.bfloat16).astype(jnp.float32)
    kstate = key_state.astype(jnp.float32)
    gstate = grad_state.astype(jnp.float32)
    query_out = jnp.einsum('hij,jhd->ihd', upstream, key_f) + jnp.einsum('ihe,hde->ihd', grad_f, kstate)
    key_out = jnp.einsum('hij,ihd->jhd', upstream, query_f) + jnp.einsum('jhe,hde->jhd', value_f, gstate)
    value_out = jnp.einsum('hij,ihe->jhe', attend, grad_f) + jnp.einsum('jhd,hde->jhe', key_f, gstate)
    return (query_out, key_out, value_out)

def reference(queries, keys, values, out_grad):
    group_count = TOKENS // TOK_DEV
    factor = 1.0 / math.sqrt(HEAD_DIM * TOKENS)
    shaped = (group_count, TOK_DEV, HEADS, HEAD_DIM)
    query_rows = queries.reshape(shaped)
    key_rows = keys.reshape(shaped)
    value_rows = values.reshape(shaped)
    grad_rows = out_grad.reshape(shaped)
    key_values = jnp.einsum('cthd,cthe->chde', key_rows.astype(jnp.float32), value_rows.astype(jnp.float32))
    query_grads = jnp.einsum('cthd,cthe->chde', query_rows.astype(jnp.float32), grad_rows.astype(jnp.float32))
    before = jnp.cumsum(key_values, 0) - key_values
    after = lax.optimization_barrier(jnp.sum(query_grads, 0)) - jnp.cumsum(query_grads, 0)
    query_out, key_out, value_out = lax.map(group_grads, (query_rows, key_rows, value_rows, grad_rows, before.astype(jnp.bfloat16), after.astype(jnp.bfloat16)))
    flat = (TOKENS, HEADS * HEAD_DIM)
    return ((query_out * factor).astype(jnp.bfloat16).reshape(flat), (key_out * factor).astype(jnp.bfloat16).reshape(flat), (value_out * factor).astype(jnp.bfloat16).reshape(flat))
```

```python
import functools
import math

import jax
import jax.numpy as jnp
from jax import lax
from jax.experimental import pallas as pl
from jax.experimental.pallas import tpu as pltpu
from jax.sharding import PartitionSpec as P

MESH = pl.DeviceIdType.MESH
F32 = jnp.float32
BF16 = jnp.bfloat16

HEAD_DIM = 128
NX, NZ, NCORE, NY = 4, 8, 2, 8
PLANE = NZ * NCORE
ROWS = 16
FAR_FIRST = (4, 3, 5, 2, 6, 1, 7, 0)


def dot(a, b, ca, cb):
    return lax.dot_general(a, b, (((ca,), (cb,)), ((), ())), preferred_element_type=F32)


def kernel(factor, q_hbm, k_hbm, v_hbm, g_hbm, qo_ref, ko_ref, vo_ref,
           q, k, v, g, att, kpart, vpart, qpart,
           kv_stage, kv_land, kv_pre, kv_tot, kv_totland, kv_out, kv_state,
           qg_stage, qg_land, qg_pre, qg_tot, qg_totland, qg_out, qg_state,
           in_sem, a2a_send, a2a_recv, ssem, rsem):
    tokens = q.shape[0]
    half = tokens // 2
    share = g_hbm.shape[0]
    width = q.shape[1]
    c = lax.axis_index("ctx")
    y = lax.axis_index("head")
    x, z, core = c // PLANE, (c // NCORE) % NZ, c % NCORE
    me = c % PLANE

    loads = []
    for i, (src, dst) in enumerate(((k_hbm, k), (v_hbm, v), (q_hbm, q))):
        loads.append(pltpu.make_async_copy(src, dst, in_sem.at[i]))
    loads.append(pltpu.make_async_copy(
        g_hbm.at[:, pl.ds(pl.multiple_of(y * width, width), width)],
        g.at[pl.ds(pl.multiple_of(y * share, share), share), :], in_sem.at[3]))
    for load in loads:
        load.start()

    plane_peers = []
    for d in FAR_FIRST:
        for dc in (1, 0):
            if d or dc:
                pz, pc = (z + d) % NZ, (core + dc) % NCORE
                plane_peers.append((pz, pc))
    barrier = pltpu.get_barrier_semaphore()
    count = 0
    for d in FAR_FIRST[:-1]:
        pl.semaphore_signal(barrier, inc=1, device_id=(c, (y + d) % NY), device_id_type=MESH)
        count += 1
    for pz, pc in plane_peers:
        pl.semaphore_signal(barrier, inc=1, device_id=(x * PLANE + pz * NCORE + pc, y), device_id_type=MESH)
        count += 1
    for d in (2, 1, 3):
        pl.semaphore_signal(barrier, inc=1, device_id=((c + d * PLANE) % (NX * PLANE), y), device_id_type=MESH)
        count += 1
    pl.semaphore_wait(barrier, count)

    for j in range(2):
        for d in FAR_FIRST[:-1]:
            t = (y + d) % NY
            pltpu.make_async_remote_copy(
                src_ref=g_hbm.at[:, pl.ds(pl.multiple_of(t * width + j * 256, 256), 256)],
                dst_ref=g.at[pl.ds(pl.multiple_of(y * share, share), share), pl.ds(j * 256, 256)],
                send_sem=a2a_send.at[j], recv_sem=a2a_recv.at[j],
                device_id=(c, t), device_id_type=MESH).start()

    def wait_bytes(ref, sem):
        pltpu.make_async_copy(ref, ref, sem).wait()

    def cols(h):
        return pl.ds(h * HEAD_DIM, HEAD_DIM)

    def put_stage(stage, e, b, value):
        stage[e, :, b * ROWS:(b + 1) * ROWS, :] = value.astype(BF16).reshape(NZ, ROWS, HEAD_DIM)

    def reduce_start(u, stage, land):
        for pz, pc in plane_peers:
            pltpu.make_async_remote_copy(
                src_ref=stage.at[pc, pz], dst_ref=land.at[me],
                send_sem=ssem.at[u, 0], recv_sem=rsem.at[u, 0],
                device_id=(x * PLANE + pz * NCORE + pc, y), device_id_type=MESH).start()
        land[me] = stage[core, z]

    def reduce_finish(u, land, pre, tot, totland, reverse):
        wait_bytes(land.at[pl.ds(0, PLANE - 1)], rsem.at[u, 0])
        running = jnp.zeros(tot.shape, F32)
        for i in (range(PLANE - 1, -1, -1) if reverse else range(PLANE)):
            pre[i] = running
            running = running + land[i].astype(F32)
        tot[...] = running
        for d in (2, 1, 3):
            pltpu.make_async_remote_copy(
                src_ref=tot, dst_ref=totland.at[x],
                send_sem=ssem.at[u, 1], recv_sem=rsem.at[u, 1],
                device_id=((c + d * PLANE) % (NX * PLANE), y), device_id_type=MESH).start()

    def gather_start(u, pre, tot, totland, out, state, reverse):
        wait_bytes(totland.at[pl.ds(0, NX - 1)], rsem.at[u, 1])
        totland[x] = tot[...]
        far = jnp.zeros(tot.shape, F32)
        for i in range(NX):
            use = (x < i) if reverse else (x > i)
            far = far + jnp.where(use, totland[i], 0.0)
        for i in range(PLANE):
            out[i] = (pre[i] + far).astype(BF16)
        for pz, pc in plane_peers:
            pltpu.make_async_remote_copy(
                src_ref=out.at[pz * NCORE + pc], dst_ref=state.at[core, z],
                send_sem=ssem.at[u, 2], recv_sem=rsem.at[u, 2],
                device_id=(x * PLANE + pz * NCORE + pc, y), device_id_type=MESH).start()
        state[core, z] = out[me]

    def gather_wait(u, land):
        wait_bytes(land.at[pl.ds(0, PLANE - 1)], rsem.at[u, 2])

    def take_state(state, e, b):
        return state[e, :, b * ROWS:(b + 1) * ROWS, :].reshape(HEAD_DIM, HEAD_DIM)

    row = lax.broadcasted_iota(jnp.int32, (half, half), 0)
    col = lax.broadcasted_iota(jnp.int32, (half, half), 1)
    lower, upper = row >= col, col >= row
    lo, hi = pl.ds(0, half), pl.ds(half, half)

    def masked(a, b, mask):
        return jnp.where(mask, dot(a, b, 1, 1), 0.0).astype(BF16)

    loads[0].wait()
    loads[1].wait()
    for h in range(4):
        put_stage(kv_stage, h // 2, h % 2, dot(k[:, cols(h)], v[:, cols(h)], 0, 0))
    reduce_start(0, kv_stage, kv_land)

    loads[2].wait()
    for h in range(4):
        att[h, lo, lo] = masked(k[lo, cols(h)], q[lo, cols(h)], upper)
        att[h, lo, hi] = dot(k[lo, cols(h)], q[hi, cols(h)], 1, 1).astype(BF16)
        att[h, hi, hi] = masked(k[hi, cols(h)], q[hi, cols(h)], upper)
    reduce_finish(0, kv_land, kv_pre, kv_tot, kv_totland, False)

    def query_states(j):
        wait_bytes(g.at[pl.ds(0, tokens - share), pl.ds(j * 256, 256)], a2a_recv.at[j])
        for e in range(2):
            h = 2 * j + e
            put_stage(qg_stage.at[j], e, 0, dot(q[:, cols(h)], g[:, cols(h)], 0, 0))
        reduce_start(1 + j, qg_stage.at[j], qg_land.at[j])

    def within(h):
        up00 = masked(g[lo, cols(h)], v[lo, cols(h)], lower)
        up10 = dot(g[hi, cols(h)], v[lo, cols(h)], 1, 1).astype(BF16)
        up11 = masked(g[hi, cols(h)], v[hi, cols(h)], lower)
        qpart[lo, cols(h)] = dot(up00, k[lo, cols(h)], 1, 0)
        qpart[hi, cols(h)] = dot(up10, k[lo, cols(h)], 1, 0) + dot(up11, k[hi, cols(h)], 1, 0)
        ut00 = masked(v[lo, cols(h)], g[lo, cols(h)], upper)
        ut01 = dot(v[lo, cols(h)], g[hi, cols(h)], 1, 1).astype(BF16)
        ut11 = masked(v[hi, cols(h)], g[hi, cols(h)], upper)
        kpart[lo, cols(h)] = dot(ut00, q[lo, cols(h)], 1, 0) + dot(ut01, q[hi, cols(h)], 1, 0)
        kpart[hi, cols(h)] = dot(ut11, q[hi, cols(h)], 1, 0)
        vpart[lo, cols(h)] = dot(att[h, lo, :], g[:, cols(h)], 1, 0)
        vpart[hi, cols(h)] = dot(att[h, hi, hi], g[hi, cols(h)], 1, 0)

    def finish(h):
        state = take_state(qg_state.at[h // 2], h % 2, 0)
        ko_ref[:, cols(h)] = ((kpart[:, cols(h)] + dot(v[:, cols(h)], state, 1, 1)) * factor).astype(BF16)
        vo_ref[:, cols(h)] = ((vpart[:, cols(h)] + dot(k[:, cols(h)], state, 1, 0)) * factor).astype(BF16)

    loads[3].wait()
    query_states(0)
    gather_start(0, kv_pre, kv_tot, kv_totland, kv_out, kv_state, False)
    query_states(1)
    within(0)
    within(1)
    reduce_finish(1, qg_land.at[0], qg_pre.at[0], qg_tot.at[0], qg_totland.at[0], True)
    within(2)
    within(3)
    gather_wait(0, kv_land)
    for h in range(4):
        state = take_state(kv_state, h // 2, h % 2)
        qo_ref[:, cols(h)] = ((qpart[:, cols(h)] + dot(g[:, cols(h)], state, 1, 1)) * factor).astype(BF16)
    gather_start(1, qg_pre.at[0], qg_tot.at[0], qg_totland.at[0], qg_out.at[0], qg_state.at[0], True)
    reduce_finish(2, qg_land.at[1], qg_pre.at[1], qg_tot.at[1], qg_totland.at[1], True)
    gather_wait(1, qg_land.at[0])
    finish(0)
    finish(1)
    gather_start(2, qg_pre.at[1], qg_tot.at[1], qg_totland.at[1], qg_out.at[1], qg_state.at[1], True)
    gather_wait(2, qg_land.at[1])
    finish(2)
    finish(3)

    for j in range(2):
        wait_bytes(g.at[pl.ds(0, tokens - share), pl.ds(j * 256, 256)], a2a_send.at[j])
    for u, (land, totland) in enumerate((
            (kv_land, kv_totland), (qg_land.at[0], qg_totland.at[0]), (qg_land.at[1], qg_totland.at[1]))):
        wait_bytes(land.at[pl.ds(0, PLANE - 1)], ssem.at[u, 0])
        wait_bytes(totland.at[pl.ds(0, NX - 1)], ssem.at[u, 1])
        wait_bytes(land.at[pl.ds(0, PLANE - 1)], ssem.at[u, 2])


def local(queries, keys, values, out_grad):
    tokens, width = queries.shape
    factor = 1.0 / math.sqrt(HEAD_DIM * tokens * lax.axis_size("ctx"))
    heads = width // HEAD_DIM
    vm = pltpu.VMEM

    def scan_scratch(lead, rows):
        return [
            vm((*lead, NCORE, NZ, rows, HEAD_DIM), BF16),
            vm((*lead, PLANE, rows, HEAD_DIM), BF16),
            vm((*lead, PLANE, rows, HEAD_DIM), F32),
            vm((*lead, rows, HEAD_DIM), F32),
            vm((*lead, NX, rows, HEAD_DIM), F32),
            vm((*lead, PLANE, rows, HEAD_DIM), BF16),
            vm((*lead, NCORE, NZ, rows, HEAD_DIM), BF16),
        ]

    dma = pltpu.SemaphoreType.DMA
    out = jax.ShapeDtypeStruct((tokens, width), BF16)
    return pl.pallas_call(
        functools.partial(kernel, factor),
        out_shape=(out, out, out),
        in_specs=[pl.BlockSpec(memory_space=pl.ANY)] * 4,
        out_specs=[pl.BlockSpec(memory_space=pltpu.VMEM)] * 3,
        scratch_shapes=[
            *[vm((tokens, width), BF16)] * 4,
            vm((heads, tokens, tokens), BF16),
            *[vm((tokens, width), F32)] * 3,
            *scan_scratch((), 2 * ROWS),
            *scan_scratch((2,), ROWS),
            dma((4,)), dma((2,)), dma((2,)), dma((3, 3)), dma((3, 3)),
        ],
        compiler_params=pltpu.CompilerParams(
            collective_id=0, has_side_effects=True, vmem_limit_bytes=56 * 2**20),
    )(queries, keys, values, out_grad)


def solution(mesh):
    return jax.shard_map(
        local,
        mesh=mesh,
        in_specs=(P("ctx", "head"), P("ctx", "head"), P("ctx", "head"), P(("ctx", "head"), None)),
        out_specs=(P("ctx", "head"), P("ctx", "head"), P("ctx", "head")),
        check_vma=False,
    )
```

```python
import functools
import math

import jax
import jax.numpy as jnp
from jax import lax
from jax.experimental import pallas as pl
from jax.experimental.pallas import tpu as pltpu
from jax.sharding import PartitionSpec as P

MESH = pl.DeviceIdType.MESH
F32 = jnp.float32
BF16 = jnp.bfloat16

HEAD_DIM = 128
NX, NZ, NCORE, NY = 4, 8, 2, 8
PLANE = NZ * NCORE
ROWS = 16
FAR_FIRST = (4, 3, 5, 2, 6, 1, 7, 0)
OWNERS = (6, 7, 0, 1)
CHUNKS = ((0, 256), (256, 128), (384, 128))


def dot(a, b, ca, cb):
    return lax.dot_general(a, b, (((ca,), (cb,)), ((), ())), preferred_element_type=F32)


def kernel(factor, q_hbm, k_hbm, v_hbm, g_hbm, qo_ref, ko_ref, vo_ref,
           q, k, v, g, att, kpart, vpart, qpart,
           kv_stage, kv_land, kv_pre, kv_tot, kv_totland, kv_out, kv_state,
           qg_stage, qg_land, qg_pre, qg_tot, qg_totland, qg_out, qg_state,
           last_stage, last_land, last_pre, last_tot, last_totland, last_out, last_state,
           in_sem, a2a_send, a2a_recv, ssem, rsem):
    tokens = q.shape[0]
    half = tokens // 2
    share = g_hbm.shape[0]
    width = q.shape[1]
    c = lax.axis_index("ctx")
    y = lax.axis_index("head")
    x, z, core = c // PLANE, (c // NCORE) % NZ, c % NCORE
    me = c % PLANE

    mine = jnp.int32(-1)
    for p in range(NZ):
        mine = jnp.where(me == OWNERS[p // 2] * NCORE + p % 2, p, mine)
    owner = mine >= 0
    piece = jnp.maximum(mine, 0)

    loads = []
    for i, (src, dst) in enumerate(((k_hbm, k), (v_hbm, v), (q_hbm, q))):
        loads.append(pltpu.make_async_copy(src, dst, in_sem.at[i]))
    loads.append(pltpu.make_async_copy(
        g_hbm.at[:, pl.ds(pl.multiple_of(y * width, width), width)],
        g.at[pl.ds(pl.multiple_of(y * share, share), share), :], in_sem.at[3]))
    for load in loads:
        load.start()

    plane_peers = []
    for d in FAR_FIRST:
        for dc in (1, 0):
            if d or dc:
                pz, pc = (z + d) % NZ, (core + dc) % NCORE
                plane_peers.append((pz, pc))
    barrier = pltpu.get_barrier_semaphore()
    count = 0
    for d in FAR_FIRST[:-1]:
        pl.semaphore_signal(barrier, inc=1, device_id=(c, (y + d) % NY), device_id_type=MESH)
        count += 1
    for pz, pc in plane_peers:
        pl.semaphore_signal(barrier, inc=1, device_id=(x * PLANE + pz * NCORE + pc, y), device_id_type=MESH)
        count += 1
    for d in (2, 1, 3):
        pl.semaphore_signal(barrier, inc=1, device_id=((c + d * PLANE) % (NX * PLANE), y), device_id_type=MESH)
        count += 1

    def wait_bytes(ref, sem):
        pltpu.make_async_copy(ref, ref, sem).wait()

    def cols(h):
        return pl.ds(h * HEAD_DIM, HEAD_DIM)

    def put_stage(stage, e, b, value):
        stage[e, :, b * ROWS:(b + 1) * ROWS, :] = value.astype(BF16).reshape(NZ, ROWS, HEAD_DIM)

    row = lax.broadcasted_iota(jnp.int32, (half, half), 0)
    col = lax.broadcasted_iota(jnp.int32, (half, half), 1)
    lower, upper = row >= col, col >= row
    lo, hi = pl.ds(0, half), pl.ds(half, half)

    def masked(a, b, mask):
        return jnp.where(mask, dot(a, b, 1, 1), 0.0).astype(BF16)

    loads[0].wait()
    loads[1].wait()
    for h in range(4):
        put_stage(kv_stage, h // 2, h % 2, dot(k[:, cols(h)], v[:, cols(h)], 0, 0))
    loads[2].wait()
    loads[3].wait()
    pl.semaphore_wait(barrier, count)

    for j, (at, wide) in enumerate(CHUNKS):
        for d in FAR_FIRST[:-1]:
            t = (y + d) % NY
            pltpu.make_async_remote_copy(
                src_ref=g_hbm.at[:, pl.ds(pl.multiple_of(t * width + at, HEAD_DIM), wide)],
                dst_ref=g.at[pl.ds(pl.multiple_of(y * share, share), share), pl.ds(at, wide)],
                send_sem=a2a_send.at[j], recv_sem=a2a_recv.at[j],
                device_id=(c, t), device_id_type=MESH).start()

    def a2a_wait(j, sem):
        at, wide = CHUNKS[j]
        wait_bytes(g.at[pl.ds(0, tokens - share), pl.ds(at, wide)], sem.at[j])

    def remote(src, dst, u, step, pz, pc):
        return pltpu.make_async_remote_copy(
            src_ref=src, dst_ref=dst, send_sem=ssem.at[u, step], recv_sem=rsem.at[u, step],
            device_id=(x * PLANE + pz * NCORE + pc, y), device_id_type=MESH)

    def reduce_start(u, stage, land):
        for pz, pc in plane_peers:
            remote(stage.at[pc, pz], land.at[me], u, 0, pz, pc).start()
        land[me] = stage[core, z]

    def reduce_sum(u, land, pre, tot, totland, reverse):
        running = jnp.zeros(tot.shape, F32)
        for i in (range(PLANE - 1, -1, -1) if reverse else range(PLANE)):
            pre[i] = running
            running = running + land[i].astype(F32)
        tot[...] = running
        for d in (2, 1, 3):
            pltpu.make_async_remote_copy(
                src_ref=tot, dst_ref=totland.at[x],
                send_sem=ssem.at[u, 1], recv_sem=rsem.at[u, 1],
                device_id=((c + d * PLANE) % (NX * PLANE), y), device_id_type=MESH).start()

    def reduce_finish(u, land, pre, tot, totland, reverse):
        wait_bytes(land.at[pl.ds(0, PLANE - 1)], rsem.at[u, 0])
        reduce_sum(u, land, pre, tot, totland, reverse)

    def gather_send(u, pre, tot, totland, out, dst, reverse):
        wait_bytes(totland.at[pl.ds(0, NX - 1)], rsem.at[u, 1])
        totland[x] = tot[...]
        far = jnp.zeros(tot.shape, F32)
        for i in range(NX):
            use = (x < i) if reverse else (x > i)
            far = far + jnp.where(use, totland[i], 0.0)
        for pz, pc in plane_peers:
            t = pz * NCORE + pc
            out[t] = (pre[t] + far).astype(BF16)
            remote(out.at[t], dst, u, 2, pz, pc).start()
        return (pre[me] + far).astype(BF16)

    def gather_start(u, pre, tot, totland, out, state, reverse):
        state[core, z] = gather_send(u, pre, tot, totland, out, state.at[core, z], reverse)

    def gather_wait(u, land):
        wait_bytes(land.at[pl.ds(0, PLANE - 1)], rsem.at[u, 2])

    def last_reduce_start(u, stage, land):
        for p in range(NZ):
            pz, pc = OWNERS[p // 2], p % 2

            @pl.when(mine != p)
            def _():
                remote(stage.at[p], land.at[me], u, 0, pz, pc).start()

        @pl.when(owner)
        def _():
            land[me] = stage[piece]

    def last_reduce_finish(u, land, pre, tot, totland):
        @pl.when(owner)
        def _():
            reduce_finish(u, land, pre, tot, totland, True)

    def last_gather_start(u, pre, tot, totland, out, state):
        @pl.when(owner)
        def _():
            state[piece] = gather_send(u, pre, tot, totland, out, state.at[piece], True)

    def last_wait(state, sem):
        @pl.when(owner)
        def _():
            wait_bytes(state.at[pl.ds(0, NZ - 1)], sem)

        @pl.when(jnp.logical_not(owner))
        def _():
            wait_bytes(state, sem)

    reduce_start(0, kv_stage, kv_land)

    for h in range(4):
        att[h, lo, lo] = masked(k[lo, cols(h)], q[lo, cols(h)], upper)
        att[h, lo, hi] = dot(k[lo, cols(h)], q[hi, cols(h)], 1, 1).astype(BF16)
        att[h, hi, hi] = masked(k[hi, cols(h)], q[hi, cols(h)], upper)
    reduce_finish(0, kv_land, kv_pre, kv_tot, kv_totland, False)

    def query_state(h):
        return dot(q[:, cols(h)], g[:, cols(h)], 0, 0)

    def within(h):
        up00 = masked(g[lo, cols(h)], v[lo, cols(h)], lower)
        up10 = dot(g[hi, cols(h)], v[lo, cols(h)], 1, 1).astype(BF16)
        up11 = masked(g[hi, cols(h)], v[hi, cols(h)], lower)
        qpart[lo, cols(h)] = dot(up00, k[lo, cols(h)], 1, 0)
        qpart[hi, cols(h)] = dot(up10, k[lo, cols(h)], 1, 0) + dot(up11, k[hi, cols(h)], 1, 0)
        ut00 = masked(v[lo, cols(h)], g[lo, cols(h)], upper)
        ut01 = dot(v[lo, cols(h)], g[hi, cols(h)], 1, 1).astype(BF16)
        ut11 = masked(v[hi, cols(h)], g[hi, cols(h)], upper)
        kpart[lo, cols(h)] = dot(ut00, q[lo, cols(h)], 1, 0) + dot(ut01, q[hi, cols(h)], 1, 0)
        kpart[hi, cols(h)] = dot(ut11, q[hi, cols(h)], 1, 0)
        vpart[lo, cols(h)] = dot(att[h, lo, :], g[:, cols(h)], 1, 0)
        vpart[hi, cols(h)] = dot(att[h, hi, hi], g[hi, cols(h)], 1, 0)

    def finish(h, state):
        ko_ref[:, cols(h)] = ((kpart[:, cols(h)] + dot(v[:, cols(h)], state, 1, 1)) * factor).astype(BF16)
        vo_ref[:, cols(h)] = ((vpart[:, cols(h)] + dot(k[:, cols(h)], state, 1, 0)) * factor).astype(BF16)

    def last(ref):
        return [r.at[ref] for r in (last_stage, last_land, last_pre, last_tot, last_totland, last_out, last_state)]

    a2a_wait(0, a2a_recv)
    for h in range(2):
        put_stage(qg_stage, h, 0, query_state(h))
    reduce_start(1, qg_stage, qg_land)
    gather_start(0, kv_pre, kv_tot, kv_totland, kv_out, kv_state, False)

    def last_states(i):
        a2a_wait(1 + i, a2a_recv)
        stage, land = last(i)[:2]
        stage[...] = query_state(2 + i).astype(BF16).reshape(NZ, ROWS, HEAD_DIM)
        last_reduce_start(2 + i, stage, land)

    last_states(0)
    within(0)
    last_states(1)
    reduce_finish(1, qg_land, qg_pre, qg_tot, qg_totland, True)
    within(1)
    last_reduce_finish(2, *last(0)[1:5])
    within(2)
    gather_start(1, qg_pre, qg_tot, qg_totland, qg_out, qg_state, True)
    within(3)
    last_reduce_finish(3, *last(1)[1:5])
    last_gather_start(2, *last(0)[2:])
    gather_wait(0, kv_land)
    for h in range(4):
        b = h % 2
        state = kv_state[h // 2, :, b * ROWS:(b + 1) * ROWS, :].reshape(HEAD_DIM, HEAD_DIM)
        qo_ref[:, cols(h)] = ((qpart[:, cols(h)] + dot(g[:, cols(h)], state, 1, 1)) * factor).astype(BF16)
    last_gather_start(3, *last(1)[2:])
    gather_wait(1, qg_land)
    for h in range(2):
        finish(h, qg_state[h].reshape(HEAD_DIM, HEAD_DIM))
    for i in range(2):
        last_wait(last_state.at[i], rsem.at[2 + i, 2])
        finish(2 + i, last_state[i].reshape(HEAD_DIM, HEAD_DIM))

    for j in range(3):
        a2a_wait(j, a2a_send)
    for u, (land, totland) in enumerate(((kv_land, kv_totland), (qg_land, qg_totland))):
        wait_bytes(land.at[pl.ds(0, PLANE - 1)], ssem.at[u, 0])
        wait_bytes(totland.at[pl.ds(0, NX - 1)], ssem.at[u, 1])
        wait_bytes(land.at[pl.ds(0, PLANE - 1)], ssem.at[u, 2])
    for i in range(2):
        last_wait(last_state.at[i], ssem.at[2 + i, 0])

    @pl.when(owner)
    def _():
        for i in range(2):
            wait_bytes(last_totland.at[i, pl.ds(0, NX - 1)], ssem.at[2 + i, 1])
            wait_bytes(last_land.at[i, pl.ds(0, PLANE - 1)], ssem.at[2 + i, 2])


def store(qo_ref, ko_ref, vo_ref, q_hbm, k_hbm, v_hbm, sem):
    copies = [pltpu.make_async_copy(src, dst, sem.at[i]) for i, (src, dst) in enumerate(
        ((qo_ref, q_hbm), (ko_ref, k_hbm), (vo_ref, v_hbm)))]
    for copy in copies:
        copy.start()
    for copy in copies:
        copy.wait()


def local(queries, keys, values, out_grad):
    tokens, width = queries.shape
    factor = 1.0 / math.sqrt(HEAD_DIM * tokens * lax.axis_size("ctx"))
    heads = width // HEAD_DIM
    vm = pltpu.VMEM

    def scan_scratch(lead, rows):
        return [
            vm((*lead, NCORE, NZ, rows, HEAD_DIM), BF16),
            vm((*lead, PLANE, rows, HEAD_DIM), BF16),
            vm((*lead, PLANE, rows, HEAD_DIM), F32),
            vm((*lead, rows, HEAD_DIM), F32),
            vm((*lead, NX, rows, HEAD_DIM), F32),
            vm((*lead, PLANE, rows, HEAD_DIM), BF16),
            vm((*lead, NCORE, NZ, rows, HEAD_DIM), BF16),
        ]

    dma = pltpu.SemaphoreType.DMA
    last = scan_scratch((2,), ROWS)
    for at in (0, -1):
        last[at] = vm((2, NZ, ROWS, HEAD_DIM), BF16)
    grads = pl.pallas_call(
        functools.partial(kernel, factor),
        out_shape=(vm((tokens, width), BF16),) * 3,
        in_specs=[pl.BlockSpec(memory_space=pltpu.HBM)] * 4,
        out_specs=[pl.BlockSpec(memory_space=pltpu.VMEM)] * 3,
        scratch_shapes=[
            *[vm((tokens, width), BF16)] * 4,
            vm((heads, tokens, tokens), BF16),
            *[vm((tokens, width), F32)] * 3,
            *scan_scratch((), 2 * ROWS),
            *scan_scratch((), ROWS),
            *last,
            dma((4,)), dma((3,)), dma((3,)), dma((4, 3)), dma((4, 3)),
        ],
        compiler_params=pltpu.CompilerParams(
            collective_id=0, has_side_effects=True, vmem_limit_bytes=20 * 2**20),
    )(*(pltpu.with_memory_space_constraint(a, pltpu.HBM) for a in (queries, keys, values, out_grad)))
    return pl.pallas_call(
        store,
        out_shape=(pltpu.HBM((tokens, width), BF16),) * 3,
        in_specs=[pl.BlockSpec(memory_space=pltpu.VMEM)] * 3,
        out_specs=[pl.BlockSpec(memory_space=pltpu.HBM)] * 3,
        scratch_shapes=[dma((3,))],
    )(*(pltpu.with_memory_space_constraint(a, pltpu.VMEM) for a in grads))


def solution(mesh):
    return jax.shard_map(
        local,
        mesh=mesh,
        in_specs=(P("ctx", "head"), P("ctx", "head"), P("ctx", "head"), P(("ctx", "head"), None)),
        out_specs=(P("ctx", "head"), P("ctx", "head"), P("ctx", "head")),
        check_vma=False,
    )
```

```python
import functools
import math

import jax
import jax.numpy as jnp
from jax import lax
from jax.experimental import pallas as pl
from jax.experimental.pallas import tpu as pltpu
from jax.sharding import PartitionSpec as P

MESH = pl.DeviceIdType.MESH
F32 = jnp.float32
BF16 = jnp.bfloat16

HEAD_DIM = 128
NX, NZ, NCORE, NY = 4, 8, 2, 8
PLANE = NZ * NCORE
ROWS = 16
FAR_FIRST = (4, 3, 5, 2, 6, 1, 7, 0)
OWNERS = tuple((z, core) for z in range(4) for core in range(2))
PIECES = len(OWNERS)
LAST_ROWS = HEAD_DIM // PIECES
CHUNKS = ((0, 256), (256, 128), (384, 128))


def dot(a, b, ca, cb):
    return lax.dot_general(a, b, (((ca,), (cb,)), ((), ())), preferred_element_type=F32)


def kernel(factor, q_hbm, k_hbm, v_hbm, g_hbm, qo_ref, ko_ref, vo_ref,
           q, k, v, g, att, kpart, vpart, qpart,
           kv_stage, kv_land, kv_pre, kv_tot, kv_totland, kv_out, kv_state,
           qg_stage, qg_land, qg_pre, qg_tot, qg_totland, qg_out, qg_state,
           last_stage, last_land, last_pre, last_tot, last_totland, last_out, last_state,
           in_sem, a2a_send, a2a_recv, ssem, rsem):
    tokens = q.shape[0]
    half = tokens // 2
    share = g_hbm.shape[0]
    width = q.shape[1]
    c = lax.axis_index("ctx")
    y = lax.axis_index("head")
    x, z, core = c // PLANE, (c // NCORE) % NZ, c % NCORE
    me = c % PLANE

    mine = jnp.int32(-1)
    for p, (pz, pc) in enumerate(OWNERS):
        mine = jnp.where(me == pz * NCORE + pc, p, mine)
    owner = mine >= 0
    piece = jnp.maximum(mine, 0)

    loads = []
    for i, (src, dst) in enumerate(((k_hbm, k), (v_hbm, v), (q_hbm, q))):
        loads.append(pltpu.make_async_copy(src, dst, in_sem.at[i]))
    loads.append(pltpu.make_async_copy(
        g_hbm.at[:, pl.ds(pl.multiple_of(y * width, width), width)],
        g.at[pl.ds(pl.multiple_of(y * share, share), share), :], in_sem.at[3]))
    for load in loads:
        load.start()

    plane_peers = []
    for d in FAR_FIRST:
        for dc in (1, 0):
            if d or dc:
                pz, pc = (z + d) % NZ, (core + dc) % NCORE
                plane_peers.append((pz, pc))
    barrier = pltpu.get_barrier_semaphore()
    count = 0
    for d in FAR_FIRST[:-1]:
        pl.semaphore_signal(barrier, inc=1, device_id=(c, (y + d) % NY), device_id_type=MESH)
        count += 1
    for pz, pc in plane_peers:
        pl.semaphore_signal(barrier, inc=1, device_id=(x * PLANE + pz * NCORE + pc, y), device_id_type=MESH)
        count += 1
    for d in (2, 1, 3):
        pl.semaphore_signal(barrier, inc=1, device_id=((c + d * PLANE) % (NX * PLANE), y), device_id_type=MESH)
        count += 1

    def wait_bytes(ref, sem):
        pltpu.make_async_copy(ref, ref, sem).wait()

    def cols(h):
        return pl.ds(h * HEAD_DIM, HEAD_DIM)

    def put_stage(stage, e, b, value):
        stage[e, :, b * ROWS:(b + 1) * ROWS, :] = value.astype(BF16).reshape(NZ, ROWS, HEAD_DIM)

    row = lax.broadcasted_iota(jnp.int32, (half, half), 0)
    col = lax.broadcasted_iota(jnp.int32, (half, half), 1)
    lower, upper = row >= col, col >= row
    lo, hi = pl.ds(0, half), pl.ds(half, half)

    def masked(a, b, mask):
        return jnp.where(mask, dot(a, b, 1, 1), 0.0).astype(BF16)

    loads[0].wait()
    loads[1].wait()
    for h in range(4):
        put_stage(kv_stage, h // 2, h % 2, dot(k[:, cols(h)], v[:, cols(h)], 0, 0))
    loads[2].wait()
    loads[3].wait()
    pl.semaphore_wait(barrier, count)

    for j, (at, wide) in enumerate(CHUNKS):
        for d in FAR_FIRST[:-1]:
            t = (y + d) % NY
            pltpu.make_async_remote_copy(
                src_ref=g_hbm.at[:, pl.ds(pl.multiple_of(t * width + at, HEAD_DIM), wide)],
                dst_ref=g.at[pl.ds(pl.multiple_of(y * share, share), share), pl.ds(at, wide)],
                send_sem=a2a_send.at[j], recv_sem=a2a_recv.at[j],
                device_id=(c, t), device_id_type=MESH).start()

    def a2a_wait(j, sem):
        at, wide = CHUNKS[j]
        wait_bytes(g.at[pl.ds(0, tokens - share), pl.ds(at, wide)], sem.at[j])

    def remote(src, dst, u, step, pz, pc):
        return pltpu.make_async_remote_copy(
            src_ref=src, dst_ref=dst, send_sem=ssem.at[u, step], recv_sem=rsem.at[u, step],
            device_id=(x * PLANE + pz * NCORE + pc, y), device_id_type=MESH)

    def reduce_start(u, stage, land):
        for pz, pc in plane_peers:
            remote(stage.at[pc, pz], land.at[me], u, 0, pz, pc).start()
        land[me] = stage[core, z]

    def reduce_sum(u, land, pre, tot, totland, reverse):
        running = jnp.zeros(tot.shape, F32)
        for i in (range(PLANE - 1, -1, -1) if reverse else range(PLANE)):
            pre[i] = running
            running = running + land[i].astype(F32)
        tot[...] = running
        for d in (2, 1, 3):
            pltpu.make_async_remote_copy(
                src_ref=tot, dst_ref=totland.at[x],
                send_sem=ssem.at[u, 1], recv_sem=rsem.at[u, 1],
                device_id=((c + d * PLANE) % (NX * PLANE), y), device_id_type=MESH).start()

    def reduce_finish(u, land, pre, tot, totland, reverse):
        wait_bytes(land.at[pl.ds(0, PLANE - 1)], rsem.at[u, 0])
        reduce_sum(u, land, pre, tot, totland, reverse)

    def gather_send(u, pre, tot, totland, out, dst, reverse):
        wait_bytes(totland.at[pl.ds(0, NX - 1)], rsem.at[u, 1])
        totland[x] = tot[...]
        far = jnp.zeros(tot.shape, F32)
        for i in range(NX):
            use = (x < i) if reverse else (x > i)
            far = far + jnp.where(use, totland[i], 0.0)
        for pz, pc in plane_peers:
            t = pz * NCORE + pc
            out[t] = (pre[t] + far).astype(BF16)
            remote(out.at[t], dst, u, 2, pz, pc).start()
        return (pre[me] + far).astype(BF16)

    def gather_start(u, pre, tot, totland, out, state, reverse):
        state[core, z] = gather_send(u, pre, tot, totland, out, state.at[core, z], reverse)

    def gather_wait(u, land):
        wait_bytes(land.at[pl.ds(0, PLANE - 1)], rsem.at[u, 2])

    def last_reduce_start(u, stage, land):
        for p, (pz, pc) in enumerate(OWNERS):
            @pl.when(mine != p)
            def _():
                remote(stage.at[p], land.at[me], u, 0, pz, pc).start()

        @pl.when(owner)
        def _():
            land[me] = stage[piece]

    def last_reduce_finish(u, land, pre, tot, totland):
        @pl.when(owner)
        def _():
            reduce_finish(u, land, pre, tot, totland, True)

    def last_gather_start(u, pre, tot, totland, out, state):
        @pl.when(owner)
        def _():
            state[piece] = gather_send(u, pre, tot, totland, out, state.at[piece], True)

    def last_wait(state, sem):
        @pl.when(owner)
        def _():
            wait_bytes(state.at[pl.ds(0, PIECES - 1)], sem)

        @pl.when(jnp.logical_not(owner))
        def _():
            wait_bytes(state, sem)

    reduce_start(0, kv_stage, kv_land)

    for h in range(4):
        att[h, lo, lo] = masked(k[lo, cols(h)], q[lo, cols(h)], upper)
        att[h, lo, hi] = dot(k[lo, cols(h)], q[hi, cols(h)], 1, 1).astype(BF16)
        att[h, hi, hi] = masked(k[hi, cols(h)], q[hi, cols(h)], upper)
    reduce_finish(0, kv_land, kv_pre, kv_tot, kv_totland, False)

    def query_state(h):
        return dot(q[:, cols(h)], g[:, cols(h)], 0, 0)

    def within(h):
        up00 = masked(g[lo, cols(h)], v[lo, cols(h)], lower)
        up10 = dot(g[hi, cols(h)], v[lo, cols(h)], 1, 1).astype(BF16)
        up11 = masked(g[hi, cols(h)], v[hi, cols(h)], lower)
        qpart[lo, cols(h)] = dot(up00, k[lo, cols(h)], 1, 0)
        qpart[hi, cols(h)] = dot(up10, k[lo, cols(h)], 1, 0) + dot(up11, k[hi, cols(h)], 1, 0)
        ut00 = masked(v[lo, cols(h)], g[lo, cols(h)], upper)
        ut01 = dot(v[lo, cols(h)], g[hi, cols(h)], 1, 1).astype(BF16)
        ut11 = masked(v[hi, cols(h)], g[hi, cols(h)], upper)
        kpart[lo, cols(h)] = dot(ut00, q[lo, cols(h)], 1, 0) + dot(ut01, q[hi, cols(h)], 1, 0)
        kpart[hi, cols(h)] = dot(ut11, q[hi, cols(h)], 1, 0)
        vpart[lo, cols(h)] = dot(att[h, lo, :], g[:, cols(h)], 1, 0)
        vpart[hi, cols(h)] = dot(att[h, hi, hi], g[hi, cols(h)], 1, 0)

    def finish(h, state):
        ko_ref[:, cols(h)] = ((kpart[:, cols(h)] + dot(v[:, cols(h)], state, 1, 1)) * factor).astype(BF16)
        vo_ref[:, cols(h)] = ((vpart[:, cols(h)] + dot(k[:, cols(h)], state, 1, 0)) * factor).astype(BF16)

    def last(ref):
        return [r.at[ref] for r in (last_stage, last_land, last_pre, last_tot, last_totland, last_out, last_state)]

    a2a_wait(0, a2a_recv)
    for h in range(2):
        put_stage(qg_stage, h, 0, query_state(h))
    reduce_start(1, qg_stage, qg_land)
    gather_start(0, kv_pre, kv_tot, kv_totland, kv_out, kv_state, False)

    def last_states(i):
        a2a_wait(1 + i, a2a_recv)
        stage, land = last(i)[:2]
        stage[...] = query_state(2 + i).astype(BF16).reshape(PIECES, LAST_ROWS, HEAD_DIM)
        last_reduce_start(2 + i, stage, land)

    last_states(0)
    within(0)
    last_states(1)
    reduce_finish(1, qg_land, qg_pre, qg_tot, qg_totland, True)
    within(1)
    last_reduce_finish(2, *last(0)[1:5])
    gather_start(1, qg_pre, qg_tot, qg_totland, qg_out, qg_state, True)
    last_reduce_finish(3, *last(1)[1:5])
    within(2)
    last_gather_start(2, *last(0)[2:])
    last_gather_start(3, *last(1)[2:])
    within(3)
    gather_wait(0, kv_land)
    for h in range(4):
        b = h % 2
        state = kv_state[h // 2, :, b * ROWS:(b + 1) * ROWS, :].reshape(HEAD_DIM, HEAD_DIM)
        qo_ref[:, cols(h)] = ((qpart[:, cols(h)] + dot(g[:, cols(h)], state, 1, 1)) * factor).astype(BF16)
    gather_wait(1, qg_land)
    for h in range(2):
        finish(h, qg_state[h].reshape(HEAD_DIM, HEAD_DIM))
    for i in range(2):
        last_wait(last_state.at[i], rsem.at[2 + i, 2])
        finish(2 + i, last_state[i].reshape(HEAD_DIM, HEAD_DIM))

    for j in range(3):
        a2a_wait(j, a2a_send)
    for u, (land, totland) in enumerate(((kv_land, kv_totland), (qg_land, qg_totland))):
        wait_bytes(land.at[pl.ds(0, PLANE - 1)], ssem.at[u, 0])
        wait_bytes(totland.at[pl.ds(0, NX - 1)], ssem.at[u, 1])
        wait_bytes(land.at[pl.ds(0, PLANE - 1)], ssem.at[u, 2])
    for i in range(2):
        last_wait(last_state.at[i], ssem.at[2 + i, 0])

    @pl.when(owner)
    def _():
        for i in range(2):
            wait_bytes(last_totland.at[i, pl.ds(0, NX - 1)], ssem.at[2 + i, 1])
            wait_bytes(last_land.at[i, pl.ds(0, PLANE - 1)], ssem.at[2 + i, 2])


def store(qo_ref, ko_ref, vo_ref, q_hbm, k_hbm, v_hbm, sem):
    copies = [pltpu.make_async_copy(src, dst, sem.at[i]) for i, (src, dst) in enumerate(
        ((qo_ref, q_hbm), (ko_ref, k_hbm), (vo_ref, v_hbm)))]
    for copy in copies:
        copy.start()
    for copy in copies:
        copy.wait()


def local(queries, keys, values, out_grad):
    tokens, width = queries.shape
    factor = 1.0 / math.sqrt(HEAD_DIM * tokens * lax.axis_size("ctx"))
    heads = width // HEAD_DIM
    vm = pltpu.VMEM

    def scan_scratch(lead, rows):
        return [
            vm((*lead, NCORE, NZ, rows, HEAD_DIM), BF16),
            vm((*lead, PLANE, rows, HEAD_DIM), BF16),
            vm((*lead, PLANE, rows, HEAD_DIM), F32),
            vm((*lead, rows, HEAD_DIM), F32),
            vm((*lead, NX, rows, HEAD_DIM), F32),
            vm((*lead, PLANE, rows, HEAD_DIM), BF16),
            vm((*lead, NCORE, NZ, rows, HEAD_DIM), BF16),
        ]

    dma = pltpu.SemaphoreType.DMA
    last = scan_scratch((2,), LAST_ROWS)
    for at in (0, -1):
        last[at] = vm((2, PIECES, LAST_ROWS, HEAD_DIM), BF16)
    grads = pl.pallas_call(
        functools.partial(kernel, factor),
        out_shape=(vm((tokens, width), BF16),) * 3,
        in_specs=[pl.BlockSpec(memory_space=pltpu.HBM)] * 4,
        out_specs=[pl.BlockSpec(memory_space=pltpu.VMEM)] * 3,
        scratch_shapes=[
            *[vm((tokens, width), BF16)] * 4,
            vm((heads, tokens, tokens), BF16),
            *[vm((tokens, width), F32)] * 3,
            *scan_scratch((), 2 * ROWS),
            *scan_scratch((), ROWS),
            *last,
            dma((4,)), dma((3,)), dma((3,)), dma((4, 3)), dma((4, 3)),
        ],
        compiler_params=pltpu.CompilerParams(
            collective_id=0, has_side_effects=True, vmem_limit_bytes=20 * 2**20),
    )(*(pltpu.with_memory_space_constraint(a, pltpu.HBM) for a in (queries, keys, values, out_grad)))
    return pl.pallas_call(
        store,
        out_shape=(pltpu.HBM((tokens, width), BF16),) * 3,
        in_specs=[pl.BlockSpec(memory_space=pltpu.VMEM)] * 3,
        out_specs=[pl.BlockSpec(memory_space=pltpu.HBM)] * 3,
        scratch_shapes=[dma((3,))],
    )(*(pltpu.with_memory_space_constraint(a, pltpu.VMEM) for a in grads))


def solution(mesh):
    return jax.shard_map(
        local,
        mesh=mesh,
        in_specs=(P("ctx", "head"), P("ctx", "head"), P("ctx", "head"), P(("ctx", "head"), None)),
        out_specs=(P("ctx", "head"), P("ctx", "head"), P("ctx", "head")),
        check_vma=False,
    )
```

```python
import functools
import math

import jax
import jax.numpy as jnp
from jax import lax
from jax.experimental import pallas as pl
from jax.experimental.pallas import tpu as pltpu
from jax.sharding import PartitionSpec as P

MESH = pl.DeviceIdType.MESH
F32 = jnp.float32
BF16 = jnp.bfloat16

HEAD_DIM = 128
NX, NZ, NCORE, NY = 4, 8, 2, 8
PLANE = NZ * NCORE
ROWS = 16
FAR_FIRST = (4, 3, 5, 2, 6, 1, 7, 0)
OWNERS = tuple((z, core) for z in range(4) for core in range(2))
PIECES = len(OWNERS)
LAST_ROWS = HEAD_DIM // PIECES
CHUNKS = ((0, 256), (256, 128), (384, 128))


def dot(a, b, ca, cb):
    return lax.dot_general(a, b, (((ca,), (cb,)), ((), ())), preferred_element_type=F32)


def kernel(factor, q_hbm, k_hbm, v_hbm, g_hbm, qo_ref, ko_ref, vo_ref,
           q, k, v, g, q_flip, att, kpart, vpart, qpart,
           kv_stage, kv_land, kv_pre, kv_tot, kv_totland, kv_out, kv_state,
           qg_stage, qg_land, qg_pre, qg_tot, qg_totland, qg_out, qg_state,
           last_stage, last_land, last_pre, last_tot, last_totland, last_out, last_state,
           in_sem, a2a_send, a2a_recv, ssem, rsem):
    tokens = q.shape[0]
    half = tokens // 2
    share = g_hbm.shape[0]
    width = q.shape[1]
    c = lax.axis_index("ctx")
    y = lax.axis_index("head")
    x, z, core = c // PLANE, (c // NCORE) % NZ, c % NCORE
    me = c % PLANE

    mine = jnp.int32(-1)
    for p, (pz, pc) in enumerate(OWNERS):
        mine = jnp.where(me == pz * NCORE + pc, p, mine)
    owner = mine >= 0
    piece = jnp.maximum(mine, 0)

    loads = []
    for i, (src, dst) in enumerate(((k_hbm, k), (v_hbm, v), (q_hbm, q))):
        loads.append(pltpu.make_async_copy(src, dst, in_sem.at[i]))
    loads.append(pltpu.make_async_copy(
        g_hbm.at[:, pl.ds(pl.multiple_of(y * width, width), width)],
        g.at[pl.ds(pl.multiple_of(y * share, share), share), :], in_sem.at[3]))
    for load in loads:
        load.start()

    plane_peers = []
    for d in FAR_FIRST:
        for dc in (1, 0):
            if d or dc:
                pz, pc = (z + d) % NZ, (core + dc) % NCORE
                plane_peers.append((pz, pc))
    barrier = pltpu.get_barrier_semaphore()
    count = 0
    for d in FAR_FIRST[:-1]:
        pl.semaphore_signal(barrier, inc=1, device_id=(c, (y + d) % NY), device_id_type=MESH)
        count += 1
    for pz, pc in plane_peers:
        pl.semaphore_signal(barrier, inc=1, device_id=(x * PLANE + pz * NCORE + pc, y), device_id_type=MESH)
        count += 1
    for d in (2, 1, 3):
        pl.semaphore_signal(barrier, inc=1, device_id=((c + d * PLANE) % (NX * PLANE), y), device_id_type=MESH)
        count += 1

    def wait_bytes(ref, sem):
        pltpu.make_async_copy(ref, ref, sem).wait()

    def cols(h):
        return pl.ds(h * HEAD_DIM, HEAD_DIM)

    def put_stage(stage, e, b, value):
        stage[e, :, b * ROWS:(b + 1) * ROWS, :] = value.astype(BF16).reshape(NZ, ROWS, HEAD_DIM)

    row = lax.broadcasted_iota(jnp.int32, (half, half), 0)
    col = lax.broadcasted_iota(jnp.int32, (half, half), 1)
    lower, upper = row >= col, col >= row
    lo, hi = pl.ds(0, half), pl.ds(half, half)

    def masked(a, b, mask):
        return jnp.where(mask, dot(a, b, 1, 1), 0.0).astype(BF16)

    loads[0].wait()
    loads[1].wait()
    for h in range(4):
        put_stage(kv_stage, h // 2, h % 2, dot(k[:, cols(h)], v[:, cols(h)], 0, 0))
    loads[2].wait()
    loads[3].wait()
    pl.semaphore_wait(barrier, count)

    for j, (at, wide) in enumerate(CHUNKS):
        for d in FAR_FIRST[:-1]:
            t = (y + d) % NY
            pltpu.make_async_remote_copy(
                src_ref=g_hbm.at[:, pl.ds(pl.multiple_of(t * width + at, HEAD_DIM), wide)],
                dst_ref=g.at[pl.ds(pl.multiple_of(y * share, share), share), pl.ds(at, wide)],
                send_sem=a2a_send.at[j], recv_sem=a2a_recv.at[j],
                device_id=(c, t), device_id_type=MESH).start()

    def a2a_wait(j, sem):
        at, wide = CHUNKS[j]
        wait_bytes(g.at[pl.ds(0, tokens - share), pl.ds(at, wide)], sem.at[j])

    def remote(src, dst, u, step, pz, pc):
        return pltpu.make_async_remote_copy(
            src_ref=src, dst_ref=dst, send_sem=ssem.at[u, step], recv_sem=rsem.at[u, step],
            device_id=(x * PLANE + pz * NCORE + pc, y), device_id_type=MESH)

    def reduce_start(u, stage, land):
        for pz, pc in plane_peers:
            remote(stage.at[pc, pz], land.at[me], u, 0, pz, pc).start()
        land[me] = stage[core, z]

    def reduce_sum(u, land, pre, tot, totland, reverse):
        running = jnp.zeros(tot.shape, F32)
        for i in (range(PLANE - 1, -1, -1) if reverse else range(PLANE)):
            pre[i] = running
            running = running + land[i].astype(F32)
        tot[...] = running
        for d in (2, 1, 3):
            pltpu.make_async_remote_copy(
                src_ref=tot, dst_ref=totland.at[x],
                send_sem=ssem.at[u, 1], recv_sem=rsem.at[u, 1],
                device_id=((c + d * PLANE) % (NX * PLANE), y), device_id_type=MESH).start()

    def reduce_finish(u, land, pre, tot, totland, reverse):
        wait_bytes(land.at[pl.ds(0, PLANE - 1)], rsem.at[u, 0])
        reduce_sum(u, land, pre, tot, totland, reverse)

    def gather_send(u, pre, tot, totland, out, dst, reverse):
        wait_bytes(totland.at[pl.ds(0, NX - 1)], rsem.at[u, 1])
        totland[x] = tot[...]
        far = jnp.zeros(tot.shape, F32)
        for i in range(NX):
            use = (x < i) if reverse else (x > i)
            far = far + jnp.where(use, totland[i], 0.0)
        for pz, pc in plane_peers:
            t = pz * NCORE + pc
            out[t] = (pre[t] + far).astype(BF16)
            remote(out.at[t], dst, u, 2, pz, pc).start()
        return (pre[me] + far).astype(BF16)

    def gather_start(u, pre, tot, totland, out, state, reverse):
        state[core, z] = gather_send(u, pre, tot, totland, out, state.at[core, z], reverse)

    def gather_wait(u, land):
        wait_bytes(land.at[pl.ds(0, PLANE - 1)], rsem.at[u, 2])

    def last_reduce_start(u, stage, land):
        for p, (pz, pc) in enumerate(OWNERS):
            @pl.when(mine != p)
            def _():
                remote(stage.at[p], land.at[me], u, 0, pz, pc).start()

        @pl.when(owner)
        def _():
            land[me] = stage[piece]

    def last_reduce_finish(u, land, pre, tot, totland):
        @pl.when(owner)
        def _():
            reduce_finish(u, land, pre, tot, totland, True)

    def last_gather_start(u, pre, tot, totland, out, state):
        @pl.when(owner)
        def _():
            state[piece] = gather_send(u, pre, tot, totland, out, state.at[piece], True)

    def last_wait(state, sem):
        @pl.when(owner)
        def _():
            wait_bytes(state.at[pl.ds(0, PIECES - 1)], sem)

        @pl.when(jnp.logical_not(owner))
        def _():
            wait_bytes(state, sem)

    reduce_start(0, kv_stage, kv_land)

    for h in range(4):
        att[h, lo, lo] = masked(k[lo, cols(h)], q[lo, cols(h)], upper)
        att[h, lo, hi] = dot(k[lo, cols(h)], q[hi, cols(h)], 1, 1).astype(BF16)
        att[h, hi, hi] = masked(k[hi, cols(h)], q[hi, cols(h)], upper)
    for i in range(2):
        q_flip[i] = q[:, cols(2 + i)].T
    reduce_finish(0, kv_land, kv_pre, kv_tot, kv_totland, False)

    def query_state(h):
        return dot(q[:, cols(h)], g[:, cols(h)], 0, 0)

    def within(h):
        up00 = masked(g[lo, cols(h)], v[lo, cols(h)], lower)
        up10 = dot(g[hi, cols(h)], v[lo, cols(h)], 1, 1).astype(BF16)
        up11 = masked(g[hi, cols(h)], v[hi, cols(h)], lower)
        qpart[lo, cols(h)] = dot(up00, k[lo, cols(h)], 1, 0)
        qpart[hi, cols(h)] = dot(up10, k[lo, cols(h)], 1, 0) + dot(up11, k[hi, cols(h)], 1, 0)
        ut00 = masked(v[lo, cols(h)], g[lo, cols(h)], upper)
        ut01 = dot(v[lo, cols(h)], g[hi, cols(h)], 1, 1).astype(BF16)
        ut11 = masked(v[hi, cols(h)], g[hi, cols(h)], upper)
        kpart[lo, cols(h)] = dot(ut00, q[lo, cols(h)], 1, 0) + dot(ut01, q[hi, cols(h)], 1, 0)
        kpart[hi, cols(h)] = dot(ut11, q[hi, cols(h)], 1, 0)
        vpart[lo, cols(h)] = dot(att[h, lo, :], g[:, cols(h)], 1, 0)
        vpart[hi, cols(h)] = dot(att[h, hi, hi], g[hi, cols(h)], 1, 0)

    def finish(h, state):
        ko_ref[:, cols(h)] = ((kpart[:, cols(h)] + dot(v[:, cols(h)], state, 1, 1)) * factor).astype(BF16)
        vo_ref[:, cols(h)] = ((vpart[:, cols(h)] + dot(k[:, cols(h)], state, 1, 0)) * factor).astype(BF16)

    def last(ref):
        return [r.at[ref] for r in (last_stage, last_land, last_pre, last_tot, last_totland, last_out, last_state)]

    a2a_wait(0, a2a_recv)
    for h in range(2):
        put_stage(qg_stage, h, 0, query_state(h))
    reduce_start(1, qg_stage, qg_land)
    gather_start(0, kv_pre, kv_tot, kv_totland, kv_out, kv_state, False)

    def last_states(i):
        a2a_wait(1 + i, a2a_recv)
        stage, land = last(i)[:2]
        stage[...] = dot(q_flip[i], g[:, cols(2 + i)], 1, 0).astype(BF16).reshape(PIECES, LAST_ROWS, HEAD_DIM)
        last_reduce_start(2 + i, stage, land)

    within(0)
    last_states(0)
    last_states(1)
    reduce_finish(1, qg_land, qg_pre, qg_tot, qg_totland, True)
    within(1)
    last_reduce_finish(2, *last(0)[1:5])
    last_reduce_finish(3, *last(1)[1:5])
    gather_start(1, qg_pre, qg_tot, qg_totland, qg_out, qg_state, True)
    within(2)
    last_gather_start(2, *last(0)[2:])
    last_gather_start(3, *last(1)[2:])
    within(3)
    gather_wait(0, kv_land)
    for h in range(4):
        b = h % 2
        state = kv_state[h // 2, :, b * ROWS:(b + 1) * ROWS, :].reshape(HEAD_DIM, HEAD_DIM)
        qo_ref[:, cols(h)] = ((qpart[:, cols(h)] + dot(g[:, cols(h)], state, 1, 1)) * factor).astype(BF16)
    gather_wait(1, qg_land)
    for h in range(2):
        finish(h, qg_state[h].reshape(HEAD_DIM, HEAD_DIM))
    last_wait(last_state.at[0], rsem.at[2, 2])
    finish(2, last_state[0].reshape(HEAD_DIM, HEAD_DIM))

    for j in range(3):
        a2a_wait(j, a2a_send)
    for u, (land, totland) in enumerate(((kv_land, kv_totland), (qg_land, qg_totland))):
        wait_bytes(land.at[pl.ds(0, PLANE - 1)], ssem.at[u, 0])
        wait_bytes(totland.at[pl.ds(0, NX - 1)], ssem.at[u, 1])
        wait_bytes(land.at[pl.ds(0, PLANE - 1)], ssem.at[u, 2])
    for i in range(2):
        last_wait(last_state.at[i], ssem.at[2 + i, 0])

    @pl.when(owner)
    def _():
        for i in range(2):
            wait_bytes(last_totland.at[i, pl.ds(0, NX - 1)], ssem.at[2 + i, 1])
        wait_bytes(last_land.at[0, pl.ds(0, PLANE - 1)], ssem.at[2, 2])

    last_wait(last_state.at[1], rsem.at[3, 2])
    finish(3, last_state[1].reshape(HEAD_DIM, HEAD_DIM))

    @pl.when(owner)
    def _():
        wait_bytes(last_land.at[1, pl.ds(0, PLANE - 1)], ssem.at[3, 2])


def store(qo_ref, ko_ref, vo_ref, q_hbm, k_hbm, v_hbm, sem):
    copies = [pltpu.make_async_copy(src, dst, sem.at[i]) for i, (src, dst) in enumerate(
        ((qo_ref, q_hbm), (ko_ref, k_hbm), (vo_ref, v_hbm)))]
    for copy in copies:
        copy.start()
    for copy in copies:
        copy.wait()


def local(queries, keys, values, out_grad):
    tokens, width = queries.shape
    factor = 1.0 / math.sqrt(HEAD_DIM * tokens * lax.axis_size("ctx"))
    heads = width // HEAD_DIM
    vm = pltpu.VMEM

    def scan_scratch(lead, rows):
        return [
            vm((*lead, NCORE, NZ, rows, HEAD_DIM), BF16),
            vm((*lead, PLANE, rows, HEAD_DIM), BF16),
            vm((*lead, PLANE, rows, HEAD_DIM), F32),
            vm((*lead, rows, HEAD_DIM), F32),
            vm((*lead, NX, rows, HEAD_DIM), F32),
            vm((*lead, PLANE, rows, HEAD_DIM), BF16),
            vm((*lead, NCORE, NZ, rows, HEAD_DIM), BF16),
        ]

    dma = pltpu.SemaphoreType.DMA
    last = scan_scratch((2,), LAST_ROWS)
    for at in (0, -1):
        last[at] = vm((2, PIECES, LAST_ROWS, HEAD_DIM), BF16)
    grads = pl.pallas_call(
        functools.partial(kernel, factor),
        out_shape=(vm((tokens, width), BF16),) * 3,
        in_specs=[pl.BlockSpec(memory_space=pltpu.HBM)] * 4,
        out_specs=[pl.BlockSpec(memory_space=pltpu.VMEM)] * 3,
        scratch_shapes=[
            *[vm((tokens, width), BF16)] * 4,
            vm((2, HEAD_DIM, tokens), BF16),
            vm((heads, tokens, tokens), BF16),
            *[vm((tokens, width), F32)] * 3,
            *scan_scratch((), 2 * ROWS),
            *scan_scratch((), ROWS),
            *last,
            dma((4,)), dma((3,)), dma((3,)), dma((4, 3)), dma((4, 3)),
        ],
        compiler_params=pltpu.CompilerParams(
            collective_id=0, has_side_effects=True, vmem_limit_bytes=20 * 2**20),
    )(*(pltpu.with_memory_space_constraint(a, pltpu.HBM) for a in (queries, keys, values, out_grad)))
    return pl.pallas_call(
        store,
        out_shape=(pltpu.HBM((tokens, width), BF16),) * 3,
        in_specs=[pl.BlockSpec(memory_space=pltpu.VMEM)] * 3,
        out_specs=[pl.BlockSpec(memory_space=pltpu.HBM)] * 3,
        scratch_shapes=[dma((3,))],
    )(*(pltpu.with_memory_space_constraint(a, pltpu.VMEM) for a in grads))


def solution(mesh):
    return jax.shard_map(
        local,
        mesh=mesh,
        in_specs=(P("ctx", "head"), P("ctx", "head"), P("ctx", "head"), P(("ctx", "head"), None)),
        out_specs=(P("ctx", "head"), P("ctx", "head"), P("ctx", "head")),
        check_vma=False,
    )
```

```python
import functools
import math

import jax
import jax.numpy as jnp
from jax import lax
from jax.experimental import pallas as pl
from jax.experimental.pallas import tpu as pltpu
from jax.sharding import PartitionSpec as P

MESH = pl.DeviceIdType.MESH
F32 = jnp.float32
BF16 = jnp.bfloat16

HEAD_DIM = 128
NX, NZ, NCORE, NY = 4, 8, 2, 8
PLANE = NZ * NCORE
ROWS = 16
FAR_FIRST = (4, 3, 5, 2, 6, 1, 7, 0)
OWNERS = tuple((z, core) for z in range(4) for core in range(2))
PIECES = len(OWNERS)
LAST_ROWS = HEAD_DIM // PIECES
CHUNKS = ((0, 256), (256, 128), (384, 128))


def dot(a, b, ca, cb):
    return lax.dot_general(a, b, (((ca,), (cb,)), ((), ())), preferred_element_type=F32)


def kernel(factor, q_hbm, k_hbm, v_hbm, g_hbm, qo_ref, ko_ref, vo_ref,
           q, k, v, g, q_flip, att, kpart, vpart, qpart,
           kv_stage, kv_land, kv_pre, kv_tot, kv_totland, kv_out, kv_state,
           qg_stage, qg_land, qg_pre, qg_tot, qg_totland, qg_out, qg_state,
           last_stage, last_land, last_pre, last_tot, last_totland, last_out, last_state,
           in_sem, a2a_send, a2a_recv, ssem, rsem):
    tokens = q.shape[0]
    half = tokens // 2
    share = g_hbm.shape[0]
    width = q.shape[1]
    c = lax.axis_index("ctx")
    y = lax.axis_index("head")
    x, z, core = c // PLANE, (c // NCORE) % NZ, c % NCORE
    me = c % PLANE

    mine = jnp.int32(-1)
    for p, (pz, pc) in enumerate(OWNERS):
        mine = jnp.where(me == pz * NCORE + pc, p, mine)
    owner = mine >= 0
    piece = jnp.maximum(mine, 0)

    loads = []
    for i, (src, dst) in enumerate(((k_hbm, k), (v_hbm, v), (q_hbm, q))):
        loads.append(pltpu.make_async_copy(src, dst, in_sem.at[i]))
    loads.append(pltpu.make_async_copy(
        g_hbm.at[:, pl.ds(pl.multiple_of(y * width, width), width)],
        g.at[pl.ds(pl.multiple_of(y * share, share), share), :], in_sem.at[3]))
    for load in loads:
        load.start()

    plane_peers = []
    for d in FAR_FIRST:
        for dc in (1, 0):
            if d or dc:
                pz, pc = (z + d) % NZ, (core + dc) % NCORE
                plane_peers.append((pz, pc))
    barrier = pltpu.get_barrier_semaphore()
    count = 0
    for d in FAR_FIRST[:-1]:
        pl.semaphore_signal(barrier, inc=1, device_id=(c, (y + d) % NY), device_id_type=MESH)
        count += 1
    for pz, pc in plane_peers:
        pl.semaphore_signal(barrier, inc=1, device_id=(x * PLANE + pz * NCORE + pc, y), device_id_type=MESH)
        count += 1
    for d in (2, 1, 3):
        pl.semaphore_signal(barrier, inc=1, device_id=((c + d * PLANE) % (NX * PLANE), y), device_id_type=MESH)
        count += 1

    def wait_bytes(ref, sem):
        pltpu.make_async_copy(ref, ref, sem).wait()

    def cols(h):
        return pl.ds(h * HEAD_DIM, HEAD_DIM)

    def put_stage(stage, e, b, value):
        stage[e, :, b * ROWS:(b + 1) * ROWS, :] = value.astype(BF16).reshape(NZ, ROWS, HEAD_DIM)

    row = lax.broadcasted_iota(jnp.int32, (half, half), 0)
    col = lax.broadcasted_iota(jnp.int32, (half, half), 1)
    lower, upper = row >= col, col >= row
    lo, hi = pl.ds(0, half), pl.ds(half, half)

    def masked(a, b, mask):
        return jnp.where(mask, dot(a, b, 1, 1), 0.0).astype(BF16)

    loads[0].wait()
    loads[1].wait()
    for h in range(4):
        put_stage(kv_stage, h // 2, h % 2, dot(k[:, cols(h)], v[:, cols(h)], 0, 0))
    loads[2].wait()
    loads[3].wait()
    pl.semaphore_wait(barrier, count)

    for j, (at, wide) in enumerate(CHUNKS):
        for d in FAR_FIRST[:-1]:
            t = (y + d) % NY
            pltpu.make_async_remote_copy(
                src_ref=g_hbm.at[:, pl.ds(pl.multiple_of(t * width + at, HEAD_DIM), wide)],
                dst_ref=g.at[pl.ds(pl.multiple_of(y * share, share), share), pl.ds(at, wide)],
                send_sem=a2a_send.at[j], recv_sem=a2a_recv.at[j],
                device_id=(c, t), device_id_type=MESH).start()

    def a2a_wait(j, sem):
        at, wide = CHUNKS[j]
        wait_bytes(g.at[pl.ds(0, tokens - share), pl.ds(at, wide)], sem.at[j])

    def remote(src, dst, u, step, pz, pc):
        return pltpu.make_async_remote_copy(
            src_ref=src, dst_ref=dst, send_sem=ssem.at[u, step], recv_sem=rsem.at[u, step],
            device_id=(x * PLANE + pz * NCORE + pc, y), device_id_type=MESH)

    def reduce_start(u, stage, land):
        for pz, pc in plane_peers:
            remote(stage.at[pc, pz], land.at[me], u, 0, pz, pc).start()
        land[me] = stage[core, z]

    def reduce_sum(u, land, pre, tot, totland, reverse):
        parts = [land[i].astype(F32) for i in range(PLANE)]
        while len(parts) > 1:
            parts = [m + n for m, n in zip(parts[::2], parts[1::2])]
        tot[...] = parts[0]
        for d in (2, 1, 3):
            pltpu.make_async_remote_copy(
                src_ref=tot, dst_ref=totland.at[x],
                send_sem=ssem.at[u, 1], recv_sem=rsem.at[u, 1],
                device_id=((c + d * PLANE) % (NX * PLANE), y), device_id_type=MESH).start()
        running = jnp.zeros(tot.shape, F32)
        for i in (range(PLANE - 1, -1, -1) if reverse else range(PLANE)):
            pre[i] = running
            running = running + land[i].astype(F32)

    def reduce_finish(u, land, pre, tot, totland, reverse):
        wait_bytes(land.at[pl.ds(0, PLANE - 1)], rsem.at[u, 0])
        reduce_sum(u, land, pre, tot, totland, reverse)

    def gather_send(u, pre, tot, totland, out, dst, reverse):
        wait_bytes(totland.at[pl.ds(0, NX - 1)], rsem.at[u, 1])
        totland[x] = tot[...]
        far = jnp.zeros(tot.shape, F32)
        for i in range(NX):
            use = (x < i) if reverse else (x > i)
            far = far + jnp.where(use, totland[i], 0.0)
        for pz, pc in plane_peers:
            t = pz * NCORE + pc
            out[t] = (pre[t] + far).astype(BF16)
            remote(out.at[t], dst, u, 2, pz, pc).start()
        return (pre[me] + far).astype(BF16)

    def gather_start(u, pre, tot, totland, out, state, reverse):
        state[core, z] = gather_send(u, pre, tot, totland, out, state.at[core, z], reverse)

    def gather_wait(u, land):
        wait_bytes(land.at[pl.ds(0, PLANE - 1)], rsem.at[u, 2])

    def last_reduce_start(u, stage, land):
        for p, (pz, pc) in enumerate(OWNERS):
            @pl.when(mine != p)
            def _():
                remote(stage.at[p], land.at[me], u, 0, pz, pc).start()

        @pl.when(owner)
        def _():
            land[me] = stage[piece]

    def last_reduce_finish(u, land, pre, tot, totland):
        @pl.when(owner)
        def _():
            reduce_finish(u, land, pre, tot, totland, True)

    def last_gather_start(u, pre, tot, totland, out, state):
        @pl.when(owner)
        def _():
            state[piece] = gather_send(u, pre, tot, totland, out, state.at[piece], True)

    def last_wait(state, sem):
        @pl.when(owner)
        def _():
            wait_bytes(state.at[pl.ds(0, PIECES - 1)], sem)

        @pl.when(jnp.logical_not(owner))
        def _():
            wait_bytes(state, sem)

    reduce_start(0, kv_stage, kv_land)

    for h in range(4):
        att[h, lo, lo] = masked(k[lo, cols(h)], q[lo, cols(h)], upper)
        att[h, lo, hi] = dot(k[lo, cols(h)], q[hi, cols(h)], 1, 1).astype(BF16)
        att[h, hi, hi] = masked(k[hi, cols(h)], q[hi, cols(h)], upper)
    for i in range(2):
        q_flip[i] = q[:, cols(2 + i)].T
    reduce_finish(0, kv_land, kv_pre, kv_tot, kv_totland, False)

    def query_state(h):
        return dot(q[:, cols(h)], g[:, cols(h)], 0, 0)

    def within(h):
        up00 = masked(g[lo, cols(h)], v[lo, cols(h)], lower)
        up10 = dot(g[hi, cols(h)], v[lo, cols(h)], 1, 1).astype(BF16)
        up11 = masked(g[hi, cols(h)], v[hi, cols(h)], lower)
        qpart[lo, cols(h)] = dot(up00, k[lo, cols(h)], 1, 0)
        qpart[hi, cols(h)] = dot(up10, k[lo, cols(h)], 1, 0) + dot(up11, k[hi, cols(h)], 1, 0)
        ut00 = masked(v[lo, cols(h)], g[lo, cols(h)], upper)
        ut01 = dot(v[lo, cols(h)], g[hi, cols(h)], 1, 1).astype(BF16)
        ut11 = masked(v[hi, cols(h)], g[hi, cols(h)], upper)
        kpart[lo, cols(h)] = dot(ut00, q[lo, cols(h)], 1, 0) + dot(ut01, q[hi, cols(h)], 1, 0)
        kpart[hi, cols(h)] = dot(ut11, q[hi, cols(h)], 1, 0)
        vpart[lo, cols(h)] = dot(att[h, lo, :], g[:, cols(h)], 1, 0)
        vpart[hi, cols(h)] = dot(att[h, hi, hi], g[hi, cols(h)], 1, 0)

    def finish(h, state):
        ko_ref[:, cols(h)] = ((kpart[:, cols(h)] + dot(v[:, cols(h)], state, 1, 1)) * factor).astype(BF16)
        vo_ref[:, cols(h)] = ((vpart[:, cols(h)] + dot(k[:, cols(h)], state, 1, 0)) * factor).astype(BF16)

    def last(ref):
        return [r.at[ref] for r in (last_stage, last_land, last_pre, last_tot, last_totland, last_out, last_state)]

    a2a_wait(0, a2a_recv)
    for h in range(2):
        put_stage(qg_stage, h, 0, query_state(h))
    reduce_start(1, qg_stage, qg_land)
    gather_start(0, kv_pre, kv_tot, kv_totland, kv_out, kv_state, False)

    def last_states(i):
        a2a_wait(1 + i, a2a_recv)
        stage, land = last(i)[:2]
        stage[...] = dot(q_flip[i], g[:, cols(2 + i)], 1, 0).astype(BF16).reshape(PIECES, LAST_ROWS, HEAD_DIM)
        last_reduce_start(2 + i, stage, land)

    within(0)
    last_states(0)
    last_states(1)
    reduce_finish(1, qg_land, qg_pre, qg_tot, qg_totland, True)
    within(1)
    last_reduce_finish(2, *last(0)[1:5])
    last_reduce_finish(3, *last(1)[1:5])
    gather_start(1, qg_pre, qg_tot, qg_totland, qg_out, qg_state, True)
    within(2)
    last_gather_start(2, *last(0)[2:])
    last_gather_start(3, *last(1)[2:])
    within(3)
    gather_wait(0, kv_land)
    for h in range(4):
        b = h % 2
        state = kv_state[h // 2, :, b * ROWS:(b + 1) * ROWS, :].reshape(HEAD_DIM, HEAD_DIM)
        qo_ref[:, cols(h)] = ((qpart[:, cols(h)] + dot(g[:, cols(h)], state, 1, 1)) * factor).astype(BF16)
    gather_wait(1, qg_land)
    for h in range(2):
        finish(h, qg_state[h].reshape(HEAD_DIM, HEAD_DIM))
    last_wait(last_state.at[0], rsem.at[2, 2])
    finish(2, last_state[0].reshape(HEAD_DIM, HEAD_DIM))

    for j in range(3):
        a2a_wait(j, a2a_send)
    for u, (land, totland) in enumerate(((kv_land, kv_totland), (qg_land, qg_totland))):
        wait_bytes(land.at[pl.ds(0, PLANE - 1)], ssem.at[u, 0])
        wait_bytes(totland.at[pl.ds(0, NX - 1)], ssem.at[u, 1])
        wait_bytes(land.at[pl.ds(0, PLANE - 1)], ssem.at[u, 2])
    for i in range(2):
        last_wait(last_state.at[i], ssem.at[2 + i, 0])

    @pl.when(owner)
    def _():
        for i in range(2):
            wait_bytes(last_totland.at[i, pl.ds(0, NX - 1)], ssem.at[2 + i, 1])
        wait_bytes(last_land.at[0, pl.ds(0, PLANE - 1)], ssem.at[2, 2])

    last_wait(last_state.at[1], rsem.at[3, 2])
    finish(3, last_state[1].reshape(HEAD_DIM, HEAD_DIM))

    @pl.when(owner)
    def _():
        wait_bytes(last_land.at[1, pl.ds(0, PLANE - 1)], ssem.at[3, 2])


def store(qo_ref, ko_ref, vo_ref, q_hbm, k_hbm, v_hbm, sem):
    copies = [pltpu.make_async_copy(src, dst, sem.at[i]) for i, (src, dst) in enumerate(
        ((qo_ref, q_hbm), (ko_ref, k_hbm), (vo_ref, v_hbm)))]
    for copy in copies:
        copy.start()
    for copy in copies:
        copy.wait()


def local(queries, keys, values, out_grad):
    tokens, width = queries.shape
    factor = 1.0 / math.sqrt(HEAD_DIM * tokens * lax.axis_size("ctx"))
    heads = width // HEAD_DIM
    vm = pltpu.VMEM

    def scan_scratch(lead, rows):
        return [
            vm((*lead, NCORE, NZ, rows, HEAD_DIM), BF16),
            vm((*lead, PLANE, rows, HEAD_DIM), BF16),
            vm((*lead, PLANE, rows, HEAD_DIM), F32),
            vm((*lead, rows, HEAD_DIM), F32),
            vm((*lead, NX, rows, HEAD_DIM), F32),
            vm((*lead, PLANE, rows, HEAD_DIM), BF16),
            vm((*lead, NCORE, NZ, rows, HEAD_DIM), BF16),
        ]

    dma = pltpu.SemaphoreType.DMA
    last = scan_scratch((2,), LAST_ROWS)
    for at in (0, -1):
        last[at] = vm((2, PIECES, LAST_ROWS, HEAD_DIM), BF16)
    grads = pl.pallas_call(
        functools.partial(kernel, factor),
        out_shape=(vm((tokens, width), BF16),) * 3,
        in_specs=[pl.BlockSpec(memory_space=pltpu.HBM)] * 4,
        out_specs=[pl.BlockSpec(memory_space=pltpu.VMEM)] * 3,
        scratch_shapes=[
            *[vm((tokens, width), BF16)] * 4,
            vm((2, HEAD_DIM, tokens), BF16),
            vm((heads, tokens, tokens), BF16),
            *[vm((tokens, width), F32)] * 3,
            *scan_scratch((), 2 * ROWS),
            *scan_scratch((), ROWS),
            *last,
            dma((4,)), dma((3,)), dma((3,)), dma((4, 3)), dma((4, 3)),
        ],
        compiler_params=pltpu.CompilerParams(
            collective_id=0, has_side_effects=True, vmem_limit_bytes=20 * 2**20),
    )(*(pltpu.with_memory_space_constraint(a, pltpu.HBM) for a in (queries, keys, values, out_grad)))
    return pl.pallas_call(
        store,
        out_shape=(pltpu.HBM((tokens, width), BF16),) * 3,
        in_specs=[pl.BlockSpec(memory_space=pltpu.VMEM)] * 3,
        out_specs=[pl.BlockSpec(memory_space=pltpu.HBM)] * 3,
        scratch_shapes=[dma((3,))],
    )(*(pltpu.with_memory_space_constraint(a, pltpu.VMEM) for a in grads))


def solution(mesh):
    return jax.shard_map(
        local,
        mesh=mesh,
        in_specs=(P("ctx", "head"), P("ctx", "head"), P("ctx", "head"), P(("ctx", "head"), None)),
        out_specs=(P("ctx", "head"), P("ctx", "head"), P("ctx", "head")),
        check_vma=False,
    )
```
